768 devices in a mesh: frame: 48 (over y_lo, z), height: 16 (over y_hi, x, core).
Axes of the slice: x: 4, y: 8 (y_hi: 2, y_lo: 4; y = y_hi * 4 + y_lo), z: 12, core: 2. Of those that a mesh axis runs over, the one named last changes fastest.
Arguments:
- latents: bfloat16 [48, 96, 64, 1152], P('frame', 'height'), may hold values from -30 to 30
- qkv_weight: bfloat16 [2, 1152, 1728], replicated, as said below
- out_weight: bfloat16 [2, 576, 1152], replicated, may hold values from -0.25 to 0.25
Outputs:
- result: bfloat16 [48, 96, 64, 1152], P('frame', 'height')
The draws below stay inside these ranges and needn't reach their ends.
Inputs may be any that keep to these rules, and one draw needn't show every extreme that they name: `qkv_weight`: entries lie within -0.2 to 0.2.
All inputs are finite; a program needn't handle non-finite values.
Results may differ from the reference program's by a relative error of at most 0.0095.
Values may be sent and summed in bfloat16 or wider, within the bound.
A program may use at most 64 MiB of HBM per device.

```python
import jax
import jax.numpy as jnp
from jax import lax

D = 1152
HEAD_DIM = 72
HEADS = 8
W = 64
INNER = 576
FRAMES = 48
ROWS = 96


def draw_latents(key, part):
    shape_all = (FRAMES, ROWS, W, D)
    noise_draw = jax.random.normal(jax.random.fold_in(key, 11), shape_all, jnp.float32)
    values_all = noise_draw
    return jnp.clip(values_all, -30.0, 30.0).astype(jnp.bfloat16)


def draw_qkv_weight(key, part):
    inner_width = HEADS * HEAD_DIM
    base = jax.random.normal(jax.random.fold_in(key, 21), (2, D, 3 * inner_width), jnp.float32) * D ** (-0.5)
    return jnp.clip(base, -0.2, 0.2).astype(jnp.bfloat16)


def centred(key, dims, width, reach, held_as=jnp.bfloat16):
    array = width * jax.random.normal(key, dims, jnp.float32)
    return jnp.clip(array, min=-reach, max=reach).astype(held_as)


def setup_inputs(seed: int = 0) -> dict:
    key_of = jax.random.split(jax.random.key(seed), 4)
    latents = draw_latents(jax.random.fold_in(key_of[3], 71), 0)
    qkv_weight = draw_qkv_weight(jax.random.fold_in(key_of[3], 71), 0)
    out_weight = centred(key_of[2], (2, INNER, D), INNER ** -0.5, 0.25)
    return dict(latents=latents, qkv_weight=qkv_weight, out_weight=out_weight)


def layer_norm(values):
    values = values.astype(jnp.float32)
    center = values - lax.optimization_barrier(jnp.mean(values, axis=-1, keepdims=True))
    spread = lax.optimization_barrier(jnp.mean(center * center, axis=-1, keepdims=True))
    return (center * lax.rsqrt(spread + 1e-06)).astype(jnp.bfloat16)

def project(tokens, weight):
    normed = layer_norm(tokens)
    flattened = normed.reshape(-1, normed.shape[-1])
    joined = jnp.dot(flattened, weight, preferred_element_type=jnp.float32)
    return joined.astype(jnp.bfloat16).reshape(tokens.shape[:-1] + (weight.shape[1],))

def attend(joined):
    length, batches = (joined.shape[0], joined.shape[1])
    inner_width = joined.shape[2] // 3
    head_count = inner_width // HEAD_DIM
    query_rows = joined[:, :, :inner_width].reshape(length, batches, head_count, HEAD_DIM).astype(jnp.float32)
    key_rows = joined[:, :, inner_width:2 * inner_width].reshape(length, batches, head_count, HEAD_DIM).astype(jnp.float32)
    value_rows = joined[:, :, 2 * inner_width:].reshape(length, batches, head_count, HEAD_DIM).astype(jnp.float32)
    scores = jnp.einsum('lbnd,mbnd->bnlm', query_rows, key_rows) * HEAD_DIM ** (-0.5)
    scores = scores - lax.optimization_barrier(jnp.max(scores, axis=-1, keepdims=True))
    exponent = jnp.exp(scores)
    weights = (exponent / lax.optimization_barrier(jnp.sum(exponent, axis=-1, keepdims=True))).astype(jnp.bfloat16)
    mixture = jnp.einsum('bnlm,mbnd->lbnd', weights.astype(jnp.float32), value_rows)
    return mixture.reshape(length, batches, inner_width).astype(jnp.bfloat16)

def residual(tokens, mixture, weight):
    update = jnp.dot(mixture.reshape(-1, mixture.shape[-1]), weight, preferred_element_type=jnp.float32)
    return (tokens.astype(jnp.float32) + update.reshape(tokens.shape)).astype(jnp.bfloat16)

def reference(latents, qkv_weight, out_weight):
    joined = lax.map(lambda frame_block: project(frame_block, qkv_weight[0]), latents)
    rows_att = lax.map(attend, joined)
    middle = lax.map(lambda paired: residual(paired[0], paired[1], out_weight[0]), (latents, rows_att))
    joined = lax.map(lambda frame_block: project(frame_block, qkv_weight[1]), middle)
    frames_att = lax.map(attend, jnp.transpose(joined, (1, 0, 2, 3)))
    frames_att = jnp.transpose(frames_att, (1, 0, 2, 3))
    return lax.map(lambda paired: residual(paired[0], paired[1], out_weight[1]), (middle, frames_att))
```

```python
import functools

import jax
import jax.numpy as jnp
from jax import lax
from jax.experimental import pallas as pl
from jax.experimental.pallas import tpu as pltpu
from jax.sharding import PartitionSpec as P

MESH = pl.DeviceIdType.MESH
BF16 = jnp.bfloat16
F32 = jnp.float32
HEAD_DIM = 72
SCALE = HEAD_DIM ** (-0.5)
GROUPS = (((0, 1, 2), 0), ((3,), 1), ((4, 5, 6), 2), ((7,), 3))


def layer_norm(values):
    center = values - jnp.mean(values, axis=-1, keepdims=True)
    spread = jnp.mean(center * center, axis=-1, keepdims=True)
    return (center * lax.rsqrt(spread + 1e-06)).astype(BF16)


def dot(a, b):
    return jnp.dot(a, b, preferred_element_type=F32)


def ones_where(condition):
    return jnp.where(condition, 1.0, 0.0).astype(BF16)


def iotas(rows, columns):
    shape = (rows, columns)
    return lax.broadcasted_iota(jnp.int32, shape, 0), lax.broadcasted_iota(jnp.int32, shape, 1)


def attend(q, k, v, same):
    tiles = [None] * 5
    for heads, first in GROUPS:
        window = slice(128 * first, 128 * first + 256)
        lane = lax.broadcasted_iota(jnp.int32, (1, 256), 1) + 128 * first
        masks = [
            jnp.where((lane >= HEAD_DIM * h) & (lane < HEAD_DIM * (h + 1)), 1.0, 0.0) for h in heads
        ]
        queries = q[:, window]
        stacked = jnp.concatenate([queries * m.astype(BF16) for m in masks], axis=0)
        scores = (
            lax.dot_general(
                stacked, k[:, window], (((1,), (1,)), ((), ())), preferred_element_type=F32
            )
            * SCALE
        )
        if same is not None:
            scores = jnp.where(same(*scores.shape), scores, -1e30)
        scores = scores - jnp.max(scores, axis=-1, keepdims=True)
        exponent = jnp.exp(scores)
        weights = (exponent / jnp.sum(exponent, axis=-1, keepdims=True)).astype(BF16)
        mixed = dot(weights, v[:, window])
        rows = q.shape[0]
        total = None
        for i, m in enumerate(masks):
            part = mixed[i * rows : (i + 1) * rows] * m
            total = part if total is None else total + part
        for half in range(2):
            part = total[:, 128 * half : 128 * half + 128]
            t = first + half
            tiles[t] = part if tiles[t] is None else tiles[t] + part
    return jnp.concatenate(tiles, axis=1)[:, :576].astype(BF16)


def same_row(rows, columns):
    a, b = iotas(rows, columns)
    return (a & 7) == (b & 7)


def kernel(
    lat, wqkv, wout, out,
    w0, w1, o0, o1,
    turn, back, sel, ext, unsel, unext,
    s1, r1, mid, s2, r2, qa, ka, va, qb, kb, vb, s3, r3, s4, r4,
    wsem, send1, recv1, send2, recv2, send3, recv3, send4, recv4,
):
    f, h = lax.axis_index("frame"), lax.axis_index("height")
    z, ylo = lax.rem(f, 12), lax.div(f, 12)
    yhi, xc = lax.div(h, 8), lax.rem(h, 8)
    x, c = lax.div(xc, 2), lax.rem(xc, 2)
    y = yhi * 4 + ylo
    column = y * 8 + xc

    loads = [
        pltpu.make_async_copy(wqkv.at[0], w0, wsem.at[0]),
        pltpu.make_async_copy(wout.at[0], o0, wsem.at[1]),
        pltpu.make_async_copy(wqkv.at[1], w1, wsem.at[2]),
        pltpu.make_async_copy(wout.at[1], o1, wsem.at[3]),
    ]
    for load in loads:
        load.start()

    def plane(dx, dy, dc):
        tx, ty, tc = lax.rem(x + dx, 4), lax.rem(y + dy, 8), lax.rem(c + dc, 2)
        th = lax.div(ty, 4) * 8 + tx * 2 + tc
        return (lax.rem(ty, 4) * 12 + z, th), th, ty * 8 + tx * 2 + tc

    def ring(dz):
        tz = lax.rem(z + dz, 12)
        return (ylo * 12 + tz, h), tz

    barrier = pltpu.get_barrier_semaphore()

    @pl.loop(1, 64)
    def _(o):
        device, _, _ = plane(lax.rem(lax.div(o, 2), 4), lax.div(o, 8), lax.rem(o, 2))
        pl.semaphore_signal(barrier, inc=1, device_id=device, device_id_type=MESH)

    @pl.loop(1, 12)
    def _(o):
        device, _ = ring(o)
        pl.semaphore_signal(barrier, inc=1, device_id=device, device_id_type=MESH)

    a, b = iotas(512, 512)
    turn[...] = ones_where(b == (a & 7) * 64 + (a >> 3))
    for t in range(0, 7, 2):
        wide = 256 if t < 6 else 128
        lanes = slice(128 * t, 128 * t + wide)
        rows = [lat[0, s, :, lanes] for s in range(6)]
        if t < 6:
            for first in (896, 1024):
                rows.append(
                    jnp.concatenate([lat[0, t + i, :, first : first + 128] for i in range(2)], axis=1)
                )
        else:
            rows.append(jnp.zeros((128, 128), BF16))
        packed = dot(turn[...], jnp.concatenate(rows, axis=0)).astype(BF16)
        s1[:, :, lanes] = packed.reshape(64, 8, wide)

    pl.semaphore_wait(barrier, 74)

    @pl.loop(0, 4)
    def _(k):
        @pl.loop(0, 16)
        def _(i):
            o = 15 - i
            device, _, there = plane(lax.rem(lax.div(o, 2), 4), k + 4 * lax.div(o, 8), lax.rem(o, 2))
            local = (k == 0) & (o == 0)

            @pl.when(jnp.logical_not(local))
            def _():
                pltpu.make_async_remote_copy(
                    src_ref=s1.at[there], dst_ref=r1.at[k, h],
                    send_sem=send1.at[k], recv_sem=recv1.at[k],
                    device_id=device, device_id_type=MESH,
                ).start()

            @pl.when(local)
            def _():
                pltpu.make_async_copy(s1.at[there], r1.at[k, h], recv1.at[k]).start()

    a, b = iotas(512, 512)
    back[...] = ones_where(b == (a & 63) * 8 + (a >> 6))
    a, b = iotas(96, 128)
    sel[...] = ones_where(((b & 7) < 6) & (a == (b >> 3) * 6 + (b & 7)))
    a, b = iotas(96, 768)
    place = a == ((b & 127) >> 3) * 6 + (b >> 7)
    ext[0:96, :] = ones_where(((b & 7) == 6) & place)
    ext[96:192, :] = ones_where(((b & 7) == 7) & place)
    a, b = iotas(128, 96)
    unsel[...] = ones_where(((a & 7) < 6) & (b == (a >> 3) * 6 + (a & 7)))
    a, b = iotas(768, 96)
    unext[...] = ones_where(((a & 7) >= 6) & (b == ((a & 127) >> 3) * 6 + (a >> 7)))
    va[...] = jnp.zeros_like(va)
    vb[...] = jnp.zeros_like(vb)

    def send_ring(k, source, target, send, recv):
        @pl.loop(0, 12)
        def _(i):
            o = lax.rem(i + 6, 12)
            device, tz = ring(o)

            @pl.when(o != 0)
            def _():
                pltpu.make_async_remote_copy(
                    src_ref=source.at[k, tz], dst_ref=target.at[k, z],
                    send_sem=send.at[k], recv_sem=recv.at[k],
                    device_id=device, device_id_type=MESH,
                ).start()

            @pl.when(o == 0)
            def _():
                pltpu.make_async_copy(source.at[k, tz], target.at[k, z], recv.at[k]).start()

    loads[0].wait()
    loads[1].wait()

    @pl.loop(0, 4)
    def _(k):
        pltpu.make_async_copy(r1.at[k], r1.at[k], recv1.at[k]).wait()
        got = r1[k].reshape(128, 896)
        tall = jnp.concatenate([got[:, 128 * t : 128 * t + 128] for t in range(6)], axis=0)
        end = dot(ext[...], tall)
        tokens = jnp.concatenate([dot(sel[...], got), end[0:96], end[96:192]], axis=1)
        joined = dot(layer_norm(tokens), w0[...]).astype(BF16)
        qa[...] = joined[:, 0:640]
        ka[...] = joined[:, 576:1216]
        va[:, 0:576] = joined[:, 1152:1728]
        mix = attend(qa[...], ka[...], va[...], None)
        middle = (tokens + dot(mix, o0[...])).astype(BF16)
        mid[k] = middle
        s2[k] = layer_norm(middle.astype(F32)).reshape(12, 8, 1152)
        send_ring(k, s2, r2, send2, recv2)

    loads[2].wait()

    @pl.loop(0, 4)
    def _(k):
        pltpu.make_async_copy(r2.at[k], r2.at[k], recv2.at[k]).wait()
        joined = dot(r2[k].reshape(96, 1152), w1[...]).astype(BF16)
        qb[k] = joined[:, 0:640]
        kb[k] = joined[:, 576:1216]
        vb[k, :, 0:576] = joined[:, 1152:1728]

    @pl.loop(0, 4)
    def _(k):
        mix = attend(qb[k], kb[...].reshape(384, 640), vb[...].reshape(384, 640), same_row)
        s3[k] = mix.reshape(12, 8, 576)
        send_ring(k, s3, r3, send3, recv3)

    loads[3].wait()

    @pl.loop(0, 4)
    def _(k):
        pltpu.make_async_copy(r3.at[k], r3.at[k], recv3.at[k]).wait()
        mix = r3[k].reshape(96, 576)
        result = (mid[k].astype(F32) + dot(mix, o1[...])).astype(BF16)
        main = dot(unsel[...], result[:, 0:896])
        end = dot(unext[...], result[:, 896:1152])
        sub = lax.broadcasted_iota(jnp.int32, (768, 128), 0) & 7
        end = jnp.where(sub == 6, end[:, 0:128], end[:, 128:256])
        tiles = [
            main[:, 128 * t : 128 * t + 128] + end[128 * t : 128 * t + 128] for t in range(6)
        ]
        tiles.append(main[:, 768:896])
        s4[k] = jnp.concatenate(tiles, axis=1).astype(BF16).reshape(16, 8, 896)

        @pl.loop(0, 16)
        def _(i):
            o = 15 - i
            device, th, _ = plane(
                lax.rem(lax.div(o, 2), 4), 8 - k + 4 * lax.div(o, 8), lax.rem(o, 2)
            )
            local = (k == 0) & (o == 0)

            @pl.when(jnp.logical_not(local))
            def _():
                pltpu.make_async_remote_copy(
                    src_ref=s4.at[k, th], dst_ref=r4.at[column],
                    send_sem=send4.at[k], recv_sem=recv4.at[0],
                    device_id=device, device_id_type=MESH,
                ).start()

            @pl.when(local)
            def _():
                pltpu.make_async_copy(s4.at[k, th], r4.at[column], recv4.at[0]).start()

    pltpu.make_async_copy(r4, r4, recv4.at[0]).wait()
    for t in range(0, 7, 2):
        wide = 256 if t < 6 else 128
        lanes = slice(128 * t, 128 * t + wide)
        turned = dot(back[...], r4[:, :, lanes].reshape(512, wide)).astype(BF16)
        for s in range(6):
            out[0, s, :, lanes] = turned[64 * s : 64 * s + 64]
        if t < 6:
            for i in range(2):
                part = turned[:, 128 * i : 128 * i + 128]
                out[0, t + i, :, 896:1024] = part[384:448]
                out[0, t + i, :, 1024:1152] = part[448:512]

    def sent(ref, sem):
        pltpu.make_async_copy(ref, ref, sem).wait()

    for k in range(4):
        plane_count = 15 if k == 0 else 16
        sent(r1.at[k, pl.ds(0, plane_count)], send1.at[k])
        sent(r2.at[k, pl.ds(0, 11)], send2.at[k])
        sent(r3.at[k, pl.ds(0, 11)], send3.at[k])
        sent(s4.at[k, pl.ds(0, plane_count)], send4.at[k])


def per_device(latents, qkv_weight, out_weight):
    vmem = pl.BlockSpec(memory_space=pltpu.VMEM)
    hbm = pl.BlockSpec(memory_space=pl.ANY)
    buffer = lambda *shape: pltpu.VMEM(shape, BF16)
    dma = pltpu.SemaphoreType.DMA
    return pl.pallas_call(
        kernel,
        out_shape=jax.ShapeDtypeStruct(latents.shape, BF16),
        in_specs=[vmem, hbm, hbm],
        out_specs=vmem,
        scratch_shapes=[
            buffer(1152, 1728), buffer(1152, 1728), buffer(576, 1152), buffer(576, 1152),
            buffer(512, 512), buffer(512, 512), buffer(96, 128), buffer(192, 768),
            buffer(128, 96), buffer(768, 96),
            buffer(64, 8, 896), buffer(4, 16, 8, 896), buffer(4, 96, 1152),
            buffer(4, 12, 8, 1152), buffer(4, 12, 8, 1152),
            buffer(96, 640), buffer(96, 640), buffer(96, 640),
            buffer(4, 96, 640), buffer(4, 96, 640), buffer(4, 96, 640),
            buffer(4, 12, 8, 576), buffer(4, 12, 8, 576),
            buffer(4, 16, 8, 896), buffer(64, 8, 896),
            dma((4,)), dma((4,)), dma((4,)), dma((4,)), dma((4,)), dma((4,)), dma((4,)),
            dma((4,)), dma((1,)),
        ],
        compiler_params=pltpu.CompilerParams(
            collective_id=0, has_side_effects=True, vmem_limit_bytes=56 * 2**20
        ),
        cost_estimate=pl.CostEstimate(
            flops=5_000_000_000, bytes_accessed=13_000_000, transcendentals=1_500_000
        ),
        name="axial_layer",
    )(latents, qkv_weight, out_weight)


def solution(mesh):
    return jax.shard_map(
        per_device,
        mesh=mesh,
        in_specs=(P("frame", "height", None, None), P(), P()),
        out_specs=P("frame", "height", None, None),
        check_vma=False,
    )
```

```python
import functools

import jax
import jax.numpy as jnp
from jax import lax
from jax.experimental import pallas as pl
from jax.experimental.pallas import tpu as pltpu
from jax.sharding import PartitionSpec as P

MESH = pl.DeviceIdType.MESH
BF16 = jnp.bfloat16
F32 = jnp.float32
HEAD_DIM = 72
SCALE = HEAD_DIM ** (-0.5)
GROUPS = (((0, 1, 2), 0), ((3,), 1), ((4, 5, 6), 2), ((7,), 3))


def layer_norm(values):
    center = values - jnp.mean(values, axis=-1, keepdims=True)
    spread = jnp.mean(center * center, axis=-1, keepdims=True)
    return (center * lax.rsqrt(spread + 1e-06)).astype(BF16)


def dot(a, b):
    return jnp.dot(a, b, preferred_element_type=F32)


def dot_t(a, b):
    return lax.dot_general(a, b, (((1,), (1,)), ((), ())), preferred_element_type=F32)


def ones_where(condition):
    return jnp.where(condition, 1.0, 0.0).astype(BF16)


def iotas(rows, columns):
    shape = (rows, columns)
    return lax.broadcasted_iota(jnp.int32, shape, 0), lax.broadcasted_iota(jnp.int32, shape, 1)


def attend(q, k, v, same):
    tiles = [None] * 5
    for heads, first in GROUPS:
        window = slice(128 * first, 128 * first + 256)
        lane = lax.broadcasted_iota(jnp.int32, (1, 256), 1) + 128 * first
        masks = [
            jnp.where((lane >= HEAD_DIM * h) & (lane < HEAD_DIM * (h + 1)), 1.0, 0.0) for h in heads
        ]
        queries = q[:, window]
        stacked = jnp.concatenate([queries * m.astype(BF16) for m in masks], axis=0)
        scores = dot_t(stacked, k[:, window]) * SCALE
        if same is not None:
            scores = jnp.where(same(*scores.shape), scores, -1e30)
        scores = scores - jnp.max(scores, axis=-1, keepdims=True)
        exponent = jnp.exp(scores)
        weights = (exponent / jnp.sum(exponent, axis=-1, keepdims=True)).astype(BF16)
        mixed = dot(weights, v[:, window])
        rows = q.shape[0]
        total = None
        for i, m in enumerate(masks):
            part = mixed[i * rows : (i + 1) * rows] * m
            total = part if total is None else total + part
        for half in range(2):
            part = total[:, 128 * half : 128 * half + 128]
            t = first + half
            tiles[t] = part if tiles[t] is None else tiles[t] + part
    return jnp.concatenate(tiles, axis=1).astype(BF16)


def same_row(rows, columns):
    a, b = iotas(rows, columns)
    return (a & 7) == (b & 7)


def kernel(
    lat, wqkv, wout, out,
    w0, w1, o0, o1,
    turn, back, sel, ext, unsel, unext,
    s1, r1, mid, s2, r2, qa, ka, va, qb, kb, vb, s3, r3, s4, r4, s5, r5,
    wsem, send1, recv1, send2, recv2, send3, recv3, send4, recv4, send5, recv5,
):
    f, h = lax.axis_index("frame"), lax.axis_index("height")
    z, ylo = lax.rem(f, 12), lax.div(f, 12)
    yhi, xc = lax.div(h, 8), lax.rem(h, 8)
    x, c = lax.div(xc, 2), lax.rem(xc, 2)
    y = yhi * 4 + ylo
    column = y * 8 + xc

    loads = [
        pltpu.make_async_copy(wqkv.at[0], w0, wsem.at[0]),
        pltpu.make_async_copy(wout.at[0], o0, wsem.at[1]),
        pltpu.make_async_copy(wqkv.at[1], w1, wsem.at[2]),
        pltpu.make_async_copy(wout.at[1], o1, wsem.at[3]),
    ]
    for load in loads:
        load.start()

    def plane(dx, dy, dc):
        tx, ty, tc = lax.rem(x + dx, 4), lax.rem(y + dy, 8), lax.rem(c + dc, 2)
        th = lax.div(ty, 4) * 8 + tx * 2 + tc
        return (lax.rem(ty, 4) * 12 + z, th), th, ty * 8 + tx * 2 + tc

    def ring(dz):
        tz = lax.rem(z + dz, 12)
        return (ylo * 12 + tz, h), tz

    barrier = pltpu.get_barrier_semaphore()

    @pl.loop(1, 64)
    def _(o):
        device, _, _ = plane(lax.rem(lax.div(o, 2), 4), lax.div(o, 8), lax.rem(o, 2))
        pl.semaphore_signal(barrier, inc=1, device_id=device, device_id_type=MESH)

    @pl.loop(1, 12)
    def _(o):
        device, _ = ring(o)
        pl.semaphore_signal(barrier, inc=1, device_id=device, device_id_type=MESH)

    a, b = iotas(512, 512)
    turn[...] = ones_where(b == (a & 7) * 64 + (a >> 3))
    for t in range(0, 7, 2):
        wide = 256 if t < 6 else 128
        lanes = slice(128 * t, 128 * t + wide)
        rows = [lat[0, s, :, lanes] for s in range(6)]
        if t < 6:
            for first in (896, 1024):
                rows.append(
                    jnp.concatenate([lat[0, t + i, :, first : first + 128] for i in range(2)], axis=1)
                )
        else:
            rows.append(jnp.zeros((128, 128), BF16))
        packed = dot(turn[...], jnp.concatenate(rows, axis=0)).astype(BF16)
        s1[:, :, lanes] = packed.reshape(64, 8, wide)

    pl.semaphore_wait(barrier, 74)

    @pl.loop(0, 4)
    def _(k):
        @pl.loop(0, 16)
        def _(i):
            o = 8 * lax.rem(i, 2) + 7 - lax.div(i, 2)
            device, _, there = plane(lax.rem(lax.div(o, 2), 4), k + 4 * lax.div(o, 8), lax.rem(o, 2))
            local = (k == 0) & (o == 0)

            @pl.when(jnp.logical_not(local))
            def _():
                pltpu.make_async_remote_copy(
                    src_ref=s1.at[there], dst_ref=r1.at[k, h],
                    send_sem=send1.at[k], recv_sem=recv1.at[k],
                    device_id=device, device_id_type=MESH,
                ).start()

            @pl.when(local)
            def _():
                pltpu.make_async_copy(s1.at[there], r1.at[k, h], recv1.at[k]).start()

    a, b = iotas(512, 512)
    back[...] = ones_where(b == (a & 63) * 8 + (a >> 6))
    a, b = iotas(96, 128)
    sel[...] = ones_where(((b & 7) < 6) & (a == (b >> 3) * 6 + (b & 7)))
    a, b = iotas(96, 768)
    place = a == ((b & 127) >> 3) * 6 + (b >> 7)
    ext[0:96, :] = ones_where(((b & 7) == 6) & place)
    ext[96:192, :] = ones_where(((b & 7) == 7) & place)
    a, b = iotas(128, 96)
    unsel[...] = ones_where(((a & 7) < 6) & (b == (a >> 3) * 6 + (a & 7)))
    a, b = iotas(512, 96)
    row, first, tile = a & 7, ((a & 127) >> 3) * 6, a >> 7
    unext[...] = ones_where(
        ((row == 6) & (b == first + tile)) | ((row == 7) & (tile < 2) & (b == first + 4 + tile))
    )
    for ref in (qa, ka, va):
        ref[:, 512:640] = jnp.zeros((96, 128), BF16)
    for ref in (qb, kb, vb):
        ref[:, :, 512:640] = jnp.zeros((4, 96, 128), BF16)

    def send_ring(k, source, target, send, recv):
        @pl.loop(0, 12)
        def _(i):
            near = lax.div(i + 1, 2)
            o = lax.rem(jnp.where(lax.rem(i, 2) == 1, 6 - near, 6 + near), 12)
            device, tz = ring(o)

            @pl.when(o != 0)
            def _():
                pltpu.make_async_remote_copy(
                    src_ref=source.at[k, tz], dst_ref=target.at[k, z],
                    send_sem=send.at[k], recv_sem=recv.at[k],
                    device_id=device, device_id_type=MESH,
                ).start()

            @pl.when(o == 0)
            def _():
                pltpu.make_async_copy(source.at[k, tz], target.at[k, z], recv.at[k]).start()

    def pack_mix(mix):
        main = dot(unsel[...], mix[:, 0:512])
        end = dot(unext[...], mix[:, 512:640])
        tiles = [
            main[:, 128 * t : 128 * t + 128] + end[128 * t : 128 * t + 128] for t in range(4)
        ]
        return jnp.concatenate(tiles, axis=1).astype(BF16).reshape(16, 8, 512)

    def send_owners(k, source, target, send, recv):
        @pl.loop(0, 16)
        def _(i):
            o = 8 * lax.rem(i, 2) + 7 - lax.div(i, 2)
            device, th, _ = plane(
                lax.rem(lax.div(o, 2), 4), 8 - k + 4 * lax.div(o, 8), lax.rem(o, 2)
            )
            local = (k == 0) & (o == 0)

            @pl.when(jnp.logical_not(local))
            def _():
                pltpu.make_async_remote_copy(
                    src_ref=source.at[k, th], dst_ref=target.at[column],
                    send_sem=send.at[k], recv_sem=recv.at[0],
                    device_id=device, device_id_type=MESH,
                ).start()

            @pl.when(local)
            def _():
                pltpu.make_async_copy(source.at[k, th], target.at[column], recv.at[0]).start()

    def finish(arrived, recv, weight, base, target):
        pltpu.make_async_copy(arrived, arrived, recv.at[0]).wait()
        turned = dot(back[...], arrived[...].reshape(512, 512)).astype(BF16)
        ends = [
            turned[384 + 64 * (t // 4) :, 128 * (t % 4) : 128 * (t % 4) + 128][0:64]
            for t in range(6)
        ]
        mix = jnp.concatenate([turned[0:384], jnp.concatenate(ends, axis=0)], axis=1)[:, 0:576]
        for n in range(3):
            lanes = slice(384 * n, 384 * n + 384)
            update = dot(mix, weight[:, lanes])
            for s in range(6):
                rows = base[0, s, :, lanes].astype(F32) + update[64 * s : 64 * s + 64]
                target[0, s, :, lanes] = rows.astype(BF16)

    loads[0].wait()
    loads[1].wait()

    @pl.loop(0, 4)
    def _(k):
        pltpu.make_async_copy(r1.at[k], r1.at[k], recv1.at[k]).wait()
        got = r1[k].reshape(128, 896)
        tall = jnp.concatenate([got[:, 128 * t : 128 * t + 128] for t in range(6)], axis=0)
        end = dot(ext[...], tall)
        tokens = jnp.concatenate([dot(sel[...], got), end[0:96], end[96:192]], axis=1)
        normed = layer_norm(tokens)
        for part, ref in enumerate((qa, ka, va)):
            ref[:, 0:576] = dot_t(normed, w0[576 * part : 576 * part + 576]).astype(BF16)
        mix = attend(qa[...], ka[...], va[...], None)
        middle = (tokens + dot(mix[:, 0:576], o0[...])).astype(BF16)
        s2[k] = layer_norm(middle.astype(F32)).reshape(12, 8, 1152)
        send_ring(k, s2, r2, send2, recv2)
        s5[k] = pack_mix(mix)
        send_owners(k, s5, r5, send5, recv5)

    loads[2].wait()

    @pl.loop(0, 4)
    def _(k):
        pltpu.make_async_copy(r2.at[k], r2.at[k], recv2.at[k]).wait()
        normed = r2[k].reshape(96, 1152)
        for part, ref in enumerate((qb, kb, vb)):
            ref[k, :, 0:576] = dot_t(normed, w1[576 * part : 576 * part + 576]).astype(BF16)

    @pl.loop(0, 4)
    def _(k):
        mix = attend(qb[k], kb[...].reshape(384, 640), vb[...].reshape(384, 640), same_row)
        s3[k] = mix.reshape(12, 8, 640)
        send_ring(k, s3, r3, send3, recv3)

    finish(r5, recv5, o0, lat, mid)
    loads[3].wait()

    @pl.loop(0, 4)
    def _(k):
        pltpu.make_async_copy(r3.at[k], r3.at[k], recv3.at[k]).wait()
        s4[k] = pack_mix(r3[k].reshape(96, 640))
        send_owners(k, s4, r4, send4, recv4)

    finish(r4, recv4, o1, mid, out)

    def sent(ref, sem):
        pltpu.make_async_copy(ref, ref, sem).wait()

    for k in range(4):
        plane_count = 15 if k == 0 else 16
        sent(r1.at[k, pl.ds(0, plane_count)], send1.at[k])
        sent(r2.at[k, pl.ds(0, 11)], send2.at[k])
        sent(r3.at[k, pl.ds(0, 11)], send3.at[k])
        sent(s4.at[k, pl.ds(0, plane_count)], send4.at[k])
        sent(s5.at[k, pl.ds(0, plane_count)], send5.at[k])


def per_device(latents, qkv_weight, out_weight):
    vmem = pl.BlockSpec(memory_space=pltpu.VMEM)
    hbm = pl.BlockSpec(memory_space=pl.ANY)
    buffer = lambda *shape: pltpu.VMEM(shape, BF16)
    dma = pltpu.SemaphoreType.DMA
    return pl.pallas_call(
        kernel,
        out_shape=jax.ShapeDtypeStruct(latents.shape, BF16),
        in_specs=[vmem, hbm, hbm],
        out_specs=vmem,
        scratch_shapes=[
            buffer(1728, 1152), buffer(1728, 1152), buffer(576, 1152), buffer(576, 1152),
            buffer(512, 512), buffer(512, 512), buffer(96, 128), buffer(192, 768),
            buffer(128, 96), buffer(512, 96),
            buffer(64, 8, 896), buffer(4, 16, 8, 896), buffer(1, 6, 64, 1152),
            buffer(4, 12, 8, 1152), buffer(4, 12, 8, 1152),
            buffer(96, 640), buffer(96, 640), buffer(96, 640),
            buffer(4, 96, 640), buffer(4, 96, 640), buffer(4, 96, 640),
            buffer(4, 12, 8, 640), buffer(4, 12, 8, 640),
            buffer(4, 16, 8, 512), buffer(64, 8, 512), buffer(4, 16, 8, 512), buffer(64, 8, 512),
            dma((4,)), dma((4,)), dma((4,)), dma((4,)), dma((4,)), dma((4,)), dma((4,)),
            dma((4,)), dma((1,)), dma((4,)), dma((1,)),
        ],
        compiler_params=pltpu.CompilerParams(
            collective_id=0, has_side_effects=True, vmem_limit_bytes=56 * 2**20
        ),
        cost_estimate=pl.CostEstimate(
            flops=5_000_000_000, bytes_accessed=13_000_000, transcendentals=1_500_000
        ),
        name="axial_layer",
    )(latents, jnp.swapaxes(qkv_weight, 1, 2), out_weight)


def solution(mesh):
    return jax.shard_map(
        per_device,
        mesh=mesh,
        in_specs=(P("frame", "height", None, None), P(), P()),
        out_specs=P("frame", "height", None, None),
        check_vma=False,
    )
```

```python
import functools

import jax
import jax.numpy as jnp
from jax import lax
from jax.experimental import pallas as pl
from jax.experimental.pallas import tpu as pltpu
from jax.sharding import PartitionSpec as P

MESH = pl.DeviceIdType.MESH
BF16 = jnp.bfloat16
F32 = jnp.float32
HEAD_DIM = 72
SCALE = HEAD_DIM ** (-0.5)
GROUPS = (((0, 1, 2), 0), ((3,), 1), ((4, 5, 6), 2), ((7,), 3))


def layer_norm(values):
    center = values - jnp.mean(values, axis=-1, keepdims=True)
    spread = jnp.mean(center * center, axis=-1, keepdims=True)
    return (center * lax.rsqrt(spread + 1e-06)).astype(BF16)


def dot(a, b):
    return jnp.dot(a, b, preferred_element_type=F32)


def dot_t(a, b):
    return lax.dot_general(a, b, (((1,), (1,)), ((), ())), preferred_element_type=F32)


def ones_where(condition):
    return jnp.where(condition, 1.0, 0.0).astype(BF16)


def iotas(rows, columns):
    shape = (rows, columns)
    return lax.broadcasted_iota(jnp.int32, shape, 0), lax.broadcasted_iota(jnp.int32, shape, 1)


def attend(q, k, v, same):
    tiles = [None] * 5
    for heads, first in GROUPS:
        window = slice(128 * first, 128 * first + 256)
        lane = lax.broadcasted_iota(jnp.int32, (1, 256), 1) + 128 * first
        masks = [
            jnp.where((lane >= HEAD_DIM * h) & (lane < HEAD_DIM * (h + 1)), 1.0, 0.0) for h in heads
        ]
        queries = q[:, window]
        stacked = jnp.concatenate([queries * m.astype(BF16) for m in masks], axis=0)
        scores = dot_t(stacked, k[:, window]) * SCALE
        if same is not None:
            scores = jnp.where(same(*scores.shape), scores, -1e30)
        scores = scores - jnp.max(scores, axis=-1, keepdims=True)
        exponent = jnp.exp(scores)
        weights = (exponent / jnp.sum(exponent, axis=-1, keepdims=True)).astype(BF16)
        mixed = dot(weights, v[:, window])
        rows = q.shape[0]
        total = None
        for i, m in enumerate(masks):
            part = mixed[i * rows : (i + 1) * rows] * m
            total = part if total is None else total + part
        for half in range(2):
            part = total[:, 128 * half : 128 * half + 128]
            t = first + half
            tiles[t] = part if tiles[t] is None else tiles[t] + part
    return jnp.concatenate(tiles, axis=1).astype(BF16)


def same_row(rows, columns):
    a, b = iotas(rows, columns)
    return (a & 7) == (b & 7)


def kernel(
    lat_hbm, wqkv, wout, out,
    lat, result, w0, w1, o0, o1,
    turn, back, sel, ext, unsel, unext,
    s1, r1, mid, s2, r2, qa, ka, va, qb, kb, vb, s3, r3, s4, r4, s5, r5,
    wsem, osem, send1, recv1, send2, recv2, send3, recv3, send4, recv4, send5, recv5,
):
    f, h = lax.axis_index("frame"), lax.axis_index("height")
    z, ylo = lax.rem(f, 12), lax.div(f, 12)
    yhi, xc = lax.div(h, 8), lax.rem(h, 8)
    x, c = lax.div(xc, 2), lax.rem(xc, 2)
    y = yhi * 4 + ylo
    column = y * 8 + xc

    entry = pltpu.make_async_copy(lat_hbm, lat, wsem.at[4])
    entry.start()
    loads = [
        pltpu.make_async_copy(wqkv.at[0], w0, wsem.at[0]),
        pltpu.make_async_copy(wout.at[0], o0, wsem.at[1]),
        pltpu.make_async_copy(wqkv.at[1], w1, wsem.at[2]),
        pltpu.make_async_copy(wout.at[1], o1, wsem.at[3]),
    ]
    across = [lax.rem(x + dx, 4) * 2 + lax.rem(c + dc, 2) for dx in range(4) for dc in range(2)]
    around = [lax.rem(z + dz, 12) for dz in range(12)]

    def level(dy):
        ty = lax.rem(y + dy, 8)
        return lax.rem(ty, 4) * 12 + z, lax.div(ty, 4) * 8, ty * 8

    barrier = pltpu.get_barrier_semaphore()
    for dy in range(8):
        frame, height, _ = level(dy)
        for i in range(8):
            if dy or i:
                pl.semaphore_signal(
                    barrier, inc=1, device_id=(frame, height + across[i]), device_id_type=MESH
                )
    for dz in range(1, 12):
        pl.semaphore_signal(
            barrier, inc=1, device_id=(ylo * 12 + around[dz], h), device_id_type=MESH
        )
    for load in loads:
        load.start()

    def send_plane(k, dy, source, target, send, recv):
        levels = [level(dy), level(dy + 4)]
        for i in range(16):
            frame, height, first = levels[i % 2]
            peer = 7 - i // 2
            block = source(height + across[peer], first + across[peer])

            def remote():
                pltpu.make_async_remote_copy(
                    src_ref=block, dst_ref=target, send_sem=send, recv_sem=recv,
                    device_id=(frame, height + across[peer]), device_id_type=MESH,
                ).start()

            if peer or i % 2:
                remote()
            else:
                pl.when(k != 0)(remote)

                @pl.when(k == 0)
                def _():
                    pltpu.make_async_copy(block, target, recv).start()

    a, b = iotas(512, 512)
    turn[...] = ones_where(b == (a & 7) * 64 + (a >> 3))
    entry.wait()
    for t in range(0, 7, 2):
        wide = 256 if t < 6 else 128
        lanes = slice(128 * t, 128 * t + wide)
        rows = [lat[0, s, :, lanes] for s in range(6)]
        if t < 6:
            for first in (896, 1024):
                rows.append(
                    jnp.concatenate([lat[0, t + i, :, first : first + 128] for i in range(2)], axis=1)
                )
        else:
            rows.append(jnp.zeros((128, 128), BF16))
        packed = dot(turn[...], jnp.concatenate(rows, axis=0)).astype(BF16)
        s1[:, :, lanes] = packed.reshape(64, 8, wide)

    pl.semaphore_wait(barrier, 74)

    @pl.loop(0, 4)
    def _(k):
        send_plane(k, k, lambda _, there: s1.at[there], r1.at[k, h], send1.at[k], recv1.at[k])

    a, b = iotas(512, 512)
    back[...] = ones_where(b == (a & 63) * 8 + (a >> 6))
    a, b = iotas(96, 128)
    sel[...] = ones_where(((b & 7) < 6) & (a == (b >> 3) * 6 + (b & 7)))
    a, b = iotas(96, 768)
    place = a == ((b & 127) >> 3) * 6 + (b >> 7)
    ext[0:96, :] = ones_where(((b & 7) == 6) & place)
    ext[96:192, :] = ones_where(((b & 7) == 7) & place)
    a, b = iotas(128, 96)
    unsel[...] = ones_where(((a & 7) < 6) & (b == (a >> 3) * 6 + (a & 7)))
    a, b = iotas(512, 96)
    row, first, tile = a & 7, ((a & 127) >> 3) * 6, a >> 7
    unext[...] = ones_where(
        ((row == 6) & (b == first + tile)) | ((row == 7) & (tile < 2) & (b == first + 4 + tile))
    )
    va[:, 512:640] = jnp.zeros((96, 128), BF16)
    vb[:, :, 512:640] = jnp.zeros((4, 96, 128), BF16)

    def send_ring(k, source, target, send, recv):
        for dz in (6, 5, 7, 4, 8, 3, 9, 2, 10, 1, 11):
            pltpu.make_async_remote_copy(
                src_ref=source.at[k, around[dz]], dst_ref=target.at[k, z],
                send_sem=send.at[k], recv_sem=recv.at[k],
                device_id=(ylo * 12 + around[dz], h), device_id_type=MESH,
            ).start()
        pltpu.make_async_copy(source.at[k, z], target.at[k, z], recv.at[k]).start()

    def pack_mix(mix):
        main = dot(unsel[...], mix[:, 0:512])
        end = dot(unext[...], mix[:, 512:640])
        tiles = [
            main[:, 128 * t : 128 * t + 128] + end[128 * t : 128 * t + 128] for t in range(4)
        ]
        return jnp.concatenate(tiles, axis=1).astype(BF16).reshape(16, 8, 512)

    def send_owners(k, source, target, send, recv):
        send_plane(
            k, 8 - k, lambda there, _: source.at[k, there], target.at[column], send.at[k], recv.at[0]
        )

    exits = [
        pltpu.make_async_copy(
            result.at[:, :, :, pl.ds(384 * n, 384)], out.at[:, :, :, pl.ds(384 * n, 384)], osem.at[n]
        )
        for n in range(3)
    ]

    def finish(arrived, recv, weight, base, target, leave):
        pltpu.make_async_copy(arrived, arrived, recv.at[0]).wait()
        turned = dot(back[...], arrived[...].reshape(512, 512)).astype(BF16)
        ends = [
            turned[384 + 64 * (t // 4) :, 128 * (t % 4) : 128 * (t % 4) + 128][0:64]
            for t in range(6)
        ]
        mix = jnp.concatenate([turned[0:384], jnp.concatenate(ends, axis=0)], axis=1)[:, 0:576]
        for n in range(3):
            lanes = slice(384 * n, 384 * n + 384)
            update = dot(mix, weight[:, lanes])
            for s in range(6):
                rows = base[0, s, :, lanes].astype(F32) + update[64 * s : 64 * s + 64]
                target[0, s, :, lanes] = rows.astype(BF16)
            if leave:
                exits[n].start()

    loads[0].wait()
    loads[1].wait()

    @pl.loop(0, 4)
    def _(k):
        pltpu.make_async_copy(r1.at[k], r1.at[k], recv1.at[k]).wait()
        got = r1[k].reshape(128, 896)
        tall = jnp.concatenate([got[:, 128 * t : 128 * t + 128] for t in range(6)], axis=0)
        end = dot(ext[...], tall)
        tokens = jnp.concatenate([dot(sel[...], got), end[0:96], end[96:192]], axis=1)
        joined = dot_t(layer_norm(tokens), w0[...]).astype(BF16)
        qa[...] = joined[:, 0:640]
        ka[...] = joined[:, 576:1216]
        va[:, 0:576] = joined[:, 1152:1728]
        mix = attend(qa[...], ka[...], va[...], None)
        middle = (tokens + dot(mix[:, 0:576], o0[...])).astype(BF16)
        s2[k] = layer_norm(middle.astype(F32)).reshape(12, 8, 1152)
        send_ring(k, s2, r2, send2, recv2)
        s5[k] = pack_mix(mix)
        send_owners(k, s5, r5, send5, recv5)

    loads[2].wait()

    @pl.loop(0, 4)
    def _(k):
        pltpu.make_async_copy(r2.at[k], r2.at[k], recv2.at[k]).wait()
        joined = dot_t(r2[k].reshape(96, 1152), w1[...]).astype(BF16)
        qb[k] = joined[:, 0:640]
        kb[k] = joined[:, 576:1216]
        vb[k, :, 0:576] = joined[:, 1152:1728]

    @pl.loop(0, 4)
    def _(k):
        mix = attend(qb[k], kb[...].reshape(384, 640), vb[...].reshape(384, 640), same_row)
        s3[k] = mix.reshape(12, 8, 640)
        send_ring(k, s3, r3, send3, recv3)

    finish(r5, recv5, o0, lat, mid, False)
    loads[3].wait()

    @pl.loop(0, 4)
    def _(k):
        pltpu.make_async_copy(r3.at[k], r3.at[k], recv3.at[k]).wait()
        s4[k] = pack_mix(r3[k].reshape(96, 640))
        send_owners(k, s4, r4, send4, recv4)

    finish(r4, recv4, o1, mid, result, True)

    def sent(ref, sem):
        pltpu.make_async_copy(ref, ref, sem).wait()

    for k in range(4):
        plane_count = 15 if k == 0 else 16
        sent(r1.at[k, pl.ds(0, plane_count)], send1.at[k])
        sent(r2.at[k, pl.ds(0, 11)], send2.at[k])
        sent(r3.at[k, pl.ds(0, 11)], send3.at[k])
        sent(s4.at[k, pl.ds(0, plane_count)], send4.at[k])
        sent(s5.at[k, pl.ds(0, plane_count)], send5.at[k])
    for leaving in exits:
        leaving.wait()


def per_device(latents, qkv_weight, out_weight):
    hbm = pl.BlockSpec(memory_space=pl.ANY)
    buffer = lambda *shape: pltpu.VMEM(shape, BF16)
    dma = pltpu.SemaphoreType.DMA
    return pl.pallas_call(
        kernel,
        out_shape=jax.ShapeDtypeStruct(latents.shape, BF16),
        in_specs=[hbm, hbm, hbm],
        out_specs=hbm,
        scratch_shapes=[
            buffer(1, 6, 64, 1152), buffer(1, 6, 64, 1152),
            buffer(1728, 1152), buffer(1728, 1152), buffer(576, 1152), buffer(576, 1152),
            buffer(512, 512), buffer(512, 512), buffer(96, 128), buffer(192, 768),
            buffer(128, 96), buffer(512, 96),
            buffer(64, 8, 896), buffer(4, 16, 8, 896), buffer(1, 6, 64, 1152),
            buffer(4, 12, 8, 1152), buffer(4, 12, 8, 1152),
            buffer(96, 640), buffer(96, 640), buffer(96, 640),
            buffer(4, 96, 640), buffer(4, 96, 640), buffer(4, 96, 640),
            buffer(4, 12, 8, 640), buffer(4, 12, 8, 640),
            buffer(4, 16, 8, 512), buffer(64, 8, 512), buffer(4, 16, 8, 512), buffer(64, 8, 512),
            dma((5,)), dma((3,)),
            dma((4,)), dma((4,)), dma((4,)), dma((4,)), dma((4,)), dma((4,)),
            dma((4,)), dma((1,)), dma((4,)), dma((1,)),
        ],
        compiler_params=pltpu.CompilerParams(
            collective_id=0, has_side_effects=True, vmem_limit_bytes=56 * 2**20
        ),
        cost_estimate=pl.CostEstimate(
            flops=5_000_000_000, bytes_accessed=13_000_000, transcendentals=1_500_000
        ),
        name="axial_layer",
    )(latents, jnp.swapaxes(qkv_weight, 1, 2), out_weight)


def solution(mesh):
    return jax.shard_map(
        per_device,
        mesh=mesh,
        in_specs=(P("frame", "height", None, None), P(), P()),
        out_specs=P("frame", "height", None, None),
        check_vma=False,
    )
```

```python
import functools

import jax
import jax.numpy as jnp
from jax import lax
from jax.experimental import pallas as pl
from jax.experimental.pallas import tpu as pltpu
from jax.sharding import PartitionSpec as P

MESH = pl.DeviceIdType.MESH
BF16 = jnp.bfloat16
F32 = jnp.float32
HEAD_DIM = 72
SCALE = HEAD_DIM ** (-0.5)
GROUPS = (((0, 1, 2), 0), ((3,), 1), ((4, 5, 6), 2), ((7,), 3))


def layer_norm(values):
    center = values - jnp.mean(values, axis=-1, keepdims=True)
    spread = jnp.mean(center * center, axis=-1, keepdims=True)
    return (center * lax.rsqrt(spread + 1e-06)).astype(BF16)


def dot(a, b):
    return jnp.dot(a, b, preferred_element_type=F32)


def dot_t(a, b):
    return lax.dot_general(a, b, (((1,), (1,)), ((), ())), preferred_element_type=F32)


def ones_where(condition):
    return jnp.where(condition, 1.0, 0.0).astype(BF16)


def iotas(rows, columns):
    shape = (rows, columns)
    return lax.broadcasted_iota(jnp.int32, shape, 0), lax.broadcasted_iota(jnp.int32, shape, 1)


def attend(q, k, v, same):
    tiles = [None] * 5
    for heads, first in GROUPS:
        window = slice(128 * first, 128 * first + 256)
        lane = lax.broadcasted_iota(jnp.int32, (1, 256), 1) + 128 * first
        masks = [
            jnp.where((lane >= HEAD_DIM * h) & (lane < HEAD_DIM * (h + 1)), 1.0, 0.0) for h in heads
        ]
        queries = q[:, window]
        stacked = jnp.concatenate([queries * m.astype(BF16) for m in masks], axis=0)
        scores = dot_t(stacked, k[:, window]) * SCALE
        if same is not None:
            scores = jnp.where(same(*scores.shape), scores, -1e30)
        scores = scores - jnp.max(scores, axis=-1, keepdims=True)
        exponent = jnp.exp(scores)
        weights = (exponent * (1.0 / jnp.sum(exponent, axis=-1, keepdims=True))).astype(BF16)
        mixed = dot(weights, v[:, window])
        rows = q.shape[0]
        total = None
        for i, m in enumerate(masks):
            part = mixed[i * rows : (i + 1) * rows] * m
            total = part if total is None else total + part
        for half in range(2):
            part = total[:, 128 * half : 128 * half + 128]
            t = first + half
            tiles[t] = part if tiles[t] is None else tiles[t] + part
    return jnp.concatenate(tiles, axis=1).astype(BF16)


def same_row(rows, columns):
    a, b = iotas(rows, columns)
    return (a & 7) == (b & 7)


def kernel(
    lat_hbm, wqkv, wout, out,
    lat, result, w0, w1, o0, o1,
    turn, back, sel, ext, unsel, unext,
    s1, r1, mid, s2, r2, qa, ka, va, qb, kb, vb, s3, r3, s4, r4, s5, r5,
    wsem, osem, send1, recv1, send2, recv2, send3, recv3, send4, recv4, send5, recv5,
):
    f, h = lax.axis_index("frame"), lax.axis_index("height")
    z, ylo = lax.rem(f, 12), lax.div(f, 12)
    yhi, xc = lax.div(h, 8), lax.rem(h, 8)
    x, c = lax.div(xc, 2), lax.rem(xc, 2)
    y = yhi * 4 + ylo
    column = y * 8 + xc

    entry = pltpu.make_async_copy(lat_hbm, lat, wsem.at[4])
    entry.start()
    loads = [
        pltpu.make_async_copy(wqkv.at[0], w0, wsem.at[0]),
        pltpu.make_async_copy(wout.at[0], o0, wsem.at[1]),
        pltpu.make_async_copy(wqkv.at[1], w1, wsem.at[2]),
        pltpu.make_async_copy(wout.at[1], o1, wsem.at[3]),
    ]
    across = [lax.rem(x + dx, 4) * 2 + lax.rem(c + dc, 2) for dx in range(4) for dc in range(2)]
    around = [lax.rem(z + dz, 12) for dz in range(12)]

    def level(dy):
        ty = lax.rem(y + dy, 8)
        return lax.rem(ty, 4) * 12 + z, lax.div(ty, 4) * 8, ty * 8

    barrier = pltpu.get_barrier_semaphore()
    for dy in range(8):
        frame, height, _ = level(dy)
        for i in range(8):
            if dy or i:
                pl.semaphore_signal(
                    barrier, inc=1, device_id=(frame, height + across[i]), device_id_type=MESH
                )
    for dz in range(1, 12):
        pl.semaphore_signal(
            barrier, inc=1, device_id=(ylo * 12 + around[dz], h), device_id_type=MESH
        )
    for load in loads:
        load.start()

    def send_plane(k, dy, source, target, send, recv):
        levels = [level(dy), level(dy + 4)]
        for i in range(16):
            farther = 1 - i % 2
            frame, height, first = levels[farther]
            peer = (4, 5, 2, 6, 3, 7, 1, 0)[i // 2]
            block = source(height + across[peer], first + across[peer])

            def remote():
                pltpu.make_async_remote_copy(
                    src_ref=block, dst_ref=target, send_sem=send, recv_sem=recv,
                    device_id=(frame, height + across[peer]), device_id_type=MESH,
                ).start()

            if peer or farther:
                remote()
            else:
                pl.when(k != 0)(remote)

                @pl.when(k == 0)
                def _():
                    pltpu.make_async_copy(block, target, recv).start()

    a, b = iotas(512, 512)
    turn[...] = ones_where(b == (a & 7) * 64 + (a >> 3))
    entry.wait()
    for t in range(0, 7, 2):
        wide = 256 if t < 6 else 128
        lanes = slice(128 * t, 128 * t + wide)
        rows = [lat[0, s, :, lanes] for s in range(6)]
        if t < 6:
            for first in (896, 1024):
                rows.append(
                    jnp.concatenate([lat[0, t + i, :, first : first + 128] for i in range(2)], axis=1)
                )
        else:
            rows.append(jnp.zeros((128, 128), BF16))
        packed = dot(turn[...], jnp.concatenate(rows, axis=0)).astype(BF16)
        s1[:, :, lanes] = packed.reshape(64, 8, wide)

    pl.semaphore_wait(barrier, 74)

    @pl.loop(0, 4)
    def _(k):
        send_plane(k, k, lambda _, there: s1.at[there], r1.at[k, h], send1.at[k], recv1.at[k])

    a, b = iotas(512, 512)
    back[...] = ones_where(b == (a & 63) * 8 + (a >> 6))
    a, b = iotas(96, 128)
    sel[...] = ones_where(((b & 7) < 6) & (a == (b >> 3) * 6 + (b & 7)))
    a, b = iotas(96, 768)
    place = a == ((b & 127) >> 3) * 6 + (b >> 7)
    ext[0:96, :] = ones_where(((b & 7) == 6) & place)
    ext[96:192, :] = ones_where(((b & 7) == 7) & place)
    a, b = iotas(128, 96)
    unsel[...] = ones_where(((a & 7) < 6) & (b == (a >> 3) * 6 + (a & 7)))
    a, b = iotas(512, 96)
    row, first, tile = a & 7, ((a & 127) >> 3) * 6, a >> 7
    unext[...] = ones_where(
        ((row == 6) & (b == first + tile)) | ((row == 7) & (tile < 2) & (b == first + 4 + tile))
    )
    va[:, 512:640] = jnp.zeros((96, 128), BF16)
    vb[:, :, 512:640] = jnp.zeros((4, 96, 128), BF16)

    def send_ring(k, source, target, send, recv):
        for dz in (6, 5, 7, 4, 8, 3, 9, 2, 10, 1, 11):
            pltpu.make_async_remote_copy(
                src_ref=source.at[k, around[dz]], dst_ref=target.at[k, z],
                send_sem=send.at[k], recv_sem=recv.at[k],
                device_id=(ylo * 12 + around[dz], h), device_id_type=MESH,
            ).start()
        pltpu.make_async_copy(source.at[k, z], target.at[k, z], recv.at[k]).start()

    def pack_mix(mix):
        main = dot(unsel[...], mix[:, 0:512])
        end = dot(unext[...], mix[:, 512:640])
        tiles = [
            main[:, 128 * t : 128 * t + 128] + end[128 * t : 128 * t + 128] for t in range(4)
        ]
        return jnp.concatenate(tiles, axis=1).astype(BF16).reshape(16, 8, 512)

    def send_owners(k, source, target, send, recv):
        send_plane(
            k, 8 - k, lambda there, _: source.at[k, there], target.at[column], send.at[k], recv.at[0]
        )

    exits = [
        pltpu.make_async_copy(
            result.at[:, :, :, pl.ds(384 * n, 384)], out.at[:, :, :, pl.ds(384 * n, 384)], osem.at[n]
        )
        for n in range(3)
    ]

    def finish(arrived, recv, weight, base, target, leave):
        pltpu.make_async_copy(arrived, arrived, recv.at[0]).wait()
        turned = dot(back[...], arrived[...].reshape(512, 512)).astype(BF16)
        ends = [
            turned[384 + 64 * (t // 4) :, 128 * (t % 4) : 128 * (t % 4) + 128][0:64]
            for t in range(6)
        ]
        mix = jnp.concatenate([turned[0:384], jnp.concatenate(ends, axis=0)], axis=1)[:, 0:576]
        for n in range(3):
            lanes = slice(384 * n, 384 * n + 384)
            update = dot(mix, weight[:, lanes])
            for s in range(6):
                rows = base[0, s, :, lanes].astype(F32) + update[64 * s : 64 * s + 64]
                target[0, s, :, lanes] = rows.astype(BF16)
            if leave:
                exits[n].start()

    loads[0].wait()
    loads[1].wait()

    @pl.loop(0, 4)
    def _(k):
        pltpu.make_async_copy(r1.at[k], r1.at[k], recv1.at[k]).wait()
        got = r1[k].reshape(128, 896)
        tall = jnp.concatenate([got[:, 128 * t : 128 * t + 128] for t in range(6)], axis=0)
        end = dot(ext[...], tall)
        tokens = jnp.concatenate([dot(sel[...], got), end[0:96], end[96:192]], axis=1)
        joined = dot_t(layer_norm(tokens), w0[...]).astype(BF16)
        qa[...] = joined[:, 0:640]
        ka[...] = joined[:, 576:1216]
        va[:, 0:576] = joined[:, 1152:1728]
        mix = attend(qa[...], ka[...], va[...], None)
        middle = (tokens + dot(mix[:, 0:576], o0[...])).astype(BF16)
        s2[k] = layer_norm(middle.astype(F32)).reshape(12, 8, 1152)
        send_ring(k, s2, r2, send2, recv2)
        s5[k] = pack_mix(mix)
        send_owners(k, s5, r5, send5, recv5)

    loads[2].wait()

    @pl.loop(0, 4)
    def _(k):
        pltpu.make_async_copy(r2.at[k], r2.at[k], recv2.at[k]).wait()
        joined = dot_t(r2[k].reshape(96, 1152), w1[...]).astype(BF16)
        qb[k] = joined[:, 0:640]
        kb[k] = joined[:, 576:1216]
        vb[k, :, 0:576] = joined[:, 1152:1728]

    @pl.loop(0, 4)
    def _(k):
        mix = attend(qb[k], kb[...].reshape(384, 640), vb[...].reshape(384, 640), same_row)
        s3[k] = mix.reshape(12, 8, 640)
        send_ring(k, s3, r3, send3, recv3)

    finish(r5, recv5, o0, lat, mid, False)
    loads[3].wait()

    @pl.loop(0, 4)
    def _(k):
        pltpu.make_async_copy(r3.at[k], r3.at[k], recv3.at[k]).wait()
        s4[k] = pack_mix(r3[k].reshape(96, 640))
        send_owners(k, s4, r4, send4, recv4)

    finish(r4, recv4, o1, mid, result, True)

    def sent(ref, sem):
        pltpu.make_async_copy(ref, ref, sem).wait()

    for k in range(4):
        plane_count = 15 if k == 0 else 16
        sent(r1.at[k, pl.ds(0, plane_count)], send1.at[k])
        sent(r2.at[k, pl.ds(0, 11)], send2.at[k])
        sent(r3.at[k, pl.ds(0, 11)], send3.at[k])
        sent(s4.at[k, pl.ds(0, plane_count)], send4.at[k])
        sent(s5.at[k, pl.ds(0, plane_count)], send5.at[k])
    for leaving in exits:
        leaving.wait()


def per_device(latents, qkv_weight, out_weight):
    hbm = pl.BlockSpec(memory_space=pl.ANY)
    buffer = lambda *shape: pltpu.VMEM(shape, BF16)
    dma = pltpu.SemaphoreType.DMA
    return pl.pallas_call(
        kernel,
        out_shape=jax.ShapeDtypeStruct(latents.shape, BF16),
        in_specs=[hbm, hbm, hbm],
        out_specs=hbm,
        scratch_shapes=[
            buffer(1, 6, 64, 1152), buffer(1, 6, 64, 1152),
            buffer(1728, 1152), buffer(1728, 1152), buffer(576, 1152), buffer(576, 1152),
            buffer(512, 512), buffer(512, 512), buffer(96, 128), buffer(192, 768),
            buffer(128, 96), buffer(512, 96),
            buffer(64, 8, 896), buffer(4, 16, 8, 896), buffer(1, 6, 64, 1152),
            buffer(4, 12, 8, 1152), buffer(4, 12, 8, 1152),
            buffer(96, 640), buffer(96, 640), buffer(96, 640),
            buffer(4, 96, 640), buffer(4, 96, 640), buffer(4, 96, 640),
            buffer(4, 12, 8, 640), buffer(4, 12, 8, 640),
            buffer(4, 16, 8, 512), buffer(64, 8, 512), buffer(4, 16, 8, 512), buffer(64, 8, 512),
            dma((5,)), dma((3,)),
            dma((4,)), dma((4,)), dma((4,)), dma((4,)), dma((4,)), dma((4,)),
            dma((4,)), dma((1,)), dma((4,)), dma((1,)),
        ],
        compiler_params=pltpu.CompilerParams(
            collective_id=0, has_side_effects=True, vmem_limit_bytes=56 * 2**20
        ),
        cost_estimate=pl.CostEstimate(
            flops=5_000_000_000, bytes_accessed=13_000_000, transcendentals=1_500_000
        ),
        name="axial_layer",
    )(latents, jnp.swapaxes(qkv_weight, 1, 2), out_weight)


def solution(mesh):
    return jax.shard_map(
        per_device,
        mesh=mesh,
        in_specs=(P("frame", "height", None, None), P(), P()),
        out_specs=P("frame", "height", None, None),
        check_vma=False,
    )
```
